128 devices in a mesh: dom: 8 (over z, x_lo), shard: 16 (over x_hi, y, core).
Axes of the slice: x: 4 (x_hi: 2, x_lo: 2; x = x_hi * 2 + x_lo), y: 4, z: 4, core: 2. Of those that a mesh axis runs over, the one named last changes fastest.
Arguments:
- inputs: bfloat16 [32768, 4096], P(('dom', 'shard')), may hold values from -18 to 18
- grads_out: bfloat16 [32768, 4096], P(('dom', 'shard')), may hold values from -1 to 1
- domain_weight: bfloat16 [8, 4096, 4096], P('dom', 'shard'), may hold values from 0.099609375 to 1.8984375
- domain_ids: int32 [8], replicated, may hold values from 0 to 7, each once
- mix_weights: float32 [8], replicated, may hold values from 0.25 to 2
Outputs:
- combined: bfloat16 [4096, 4096], P('shard')
- gram: float32 [8, 8], replicated
The draws below stay inside these ranges and needn't reach their ends.
Inputs may be any that keep to these rules, and one draw needn't show every extreme that they name: `domain_ids`: each domain id appears once.
All inputs are finite; a program needn't handle non-finite values.
Results may differ from the reference program's by a relative error of at most 0.017.
Values may be sent and summed in bfloat16 or wider, within the bound.
No kernel may reach another device: no remote copies, remote signals or barrier semaphores. Data moves between devices by JAX's collectives and lax.ppermute only.
A program may use at most 128 MiB of HBM per device.

```python
import math
import jax
import jax.numpy as jnp
from jax import lax

D_IN = 4096
WIN = 4096
TOK_DEV = 256
DOMAINS = 8
ROWS = 4096
N_SHARD = 16


def shared_signs(key):
    total = DOMAINS * ROWS
    flips = jax.random.bernoulli(jax.random.fold_in(key, 7), 0.5, (total, 1))
    return jnp.where(flips, 1.0, -1.0).astype(jnp.float32)


def draw_inputs(key, part):
    signs = shared_signs(key)
    key = jax.random.fold_in(key, 1)
    key_noise, key_pair, key_common = jax.random.split(key, 3)
    total = DOMAINS * ROWS
    blocks = total // TOK_DEV
    width = D_IN // blocks
    noise = jnp.clip(jax.random.normal(key_noise, (total, D_IN), jnp.float32), -4.0, 4.0)
    strength = 0.5
    pairing = jax.random.permutation(key_pair, blocks)
    row_block = jnp.arange(total, dtype=jnp.int32) // TOK_DEV
    col_block = jnp.arange(D_IN, dtype=jnp.int32) // width
    spike = jnp.where(pairing[row_block][:, None] == col_block[None, :], 4.0, 1.0)
    common = jnp.clip(jax.random.normal(key_common, (1, D_IN), jnp.float32), -3.0, 3.0)
    return (noise * spike + strength * signs * common).astype(jnp.bfloat16)


def draw_grads_out(key, part):
    signs = shared_signs(key)
    key = jax.random.fold_in(key, 2)
    key_noise, key_common = jax.random.split(key, 2)
    total = DOMAINS * ROWS
    noise = jnp.clip(jax.random.normal(key_noise, (total, WIN), jnp.float32), -6.0, 6.0)
    strength = 2.0
    common = jnp.clip(jax.random.normal(key_common, (1, WIN), jnp.float32), -3.0, 3.0)
    values = noise * (1.0 / math.sqrt(ROWS)) + strength / ROWS * signs * common
    return values.astype(jnp.bfloat16)


def setup_inputs(seed: int = 0) -> dict:
    key_list = jax.random.split(jax.random.key(seed), 6)
    inputs = draw_inputs(jax.random.fold_in(key_list[5], 71), 0)
    grads_out = draw_grads_out(jax.random.fold_in(key_list[5], 71), 0)
    domain_weight = jnp.clip(1.0 + 0.18 * jax.random.normal(key_list[2], (DOMAINS, D_IN, WIN), jnp.float32), 0.099609375, 1.8984375).astype(jnp.bfloat16)
    domain_ids = jax.random.permutation(key_list[3], DOMAINS).astype(jnp.int32)
    mix_weights = jnp.clip(jnp.exp(jax.random.uniform(key_list[4], (DOMAINS,), jnp.float32, math.log(0.25), math.log(2.0))), 0.25, 2.0)
    return dict(inputs=inputs, grads_out=grads_out, domain_weight=domain_weight, domain_ids=domain_ids, mix_weights=mix_weights)


def reference(inputs, grads_out, domain_weight, domain_ids, mix_weights):

    def one_group(group):

        def add_block(total, block):
            start = group * ROWS + block * TOK_DEV
            left = lax.dynamic_slice_in_dim(inputs, start, TOK_DEV, 0)
            right = lax.dynamic_slice_in_dim(grads_out, start, TOK_DEV, 0)
            part = lax.dot_general(left, right, (((0,), (0,)), ((), ())), preferred_element_type=jnp.float32)
            return (total + part.astype(jnp.bfloat16).astype(jnp.float32), None)
        weff_grad, unused = lax.scan(add_block, jnp.zeros((D_IN, WIN), jnp.float32), jnp.arange(N_SHARD, dtype=jnp.int32))
        return (weff_grad * domain_weight[group].astype(jnp.float32)).astype(jnp.bfloat16)
    center_grad = lax.map(one_group, jnp.arange(DOMAINS, dtype=jnp.int32))
    flat = center_grad.reshape(DOMAINS, D_IN * WIN)
    group_gram = lax.dot_general(flat, flat, (((1,), (1,)), ((), ())), preferred_element_type=jnp.float32) / (D_IN * WIN)
    onehot = (domain_ids[:, None] == jnp.arange(DOMAINS, dtype=jnp.int32)[None, :]).astype(jnp.float32)
    hi = lax.Precision.HIGHEST
    gram = jnp.dot(jnp.dot(onehot.T, group_gram, precision=hi), onehot, precision=hi)
    weights = jnp.dot(onehot, mix_weights, precision=hi)
    scale = weights / jnp.sqrt(jnp.diagonal(group_gram) + 1e-06)

    def accumulate(total, item):
        factor, grad = item
        return (total + factor * grad.astype(jnp.float32), None)
    combined, unused = lax.scan(accumulate, jnp.zeros((D_IN, WIN), jnp.float32), (scale, center_grad))
    return (combined.astype(jnp.bfloat16), gram)
```

```python
import jax
import jax.numpy as jnp
from jax import lax
from jax.experimental import pallas as pl
from jax.experimental.pallas import tpu as pltpu
from jax.sharding import PartitionSpec as P

D_IN = 4096
WIN = 4096
AXES = ("dom", "shard")
CHUNKS = (1024, 1024, 1024, 1024)
HALF = 128
F32 = jnp.float32
BF16 = jnp.bfloat16


def device_index(x, y, z, core):
    return (z * 2 + x % 2) * 16 + (x // 2) * 8 + y * 2 + core


def shift(value, dx=0, dy=0, dz=0, pair=0, core=0):
    moves = [
        (
            device_index(x, y, z, c),
            device_index(((x ^ pair) + dx) % 4, (y + dy) % 4, (z + dz) % 4, c ^ core),
        )
        for x in range(4)
        for y in range(4)
        for z in range(4)
        for c in range(2)
    ]
    return lax.ppermute(value, AXES, moves)


def sum_everywhere(value):
    value = value + shift(value, core=1)
    for axis in ("dy", "dx", "dz"):
        near, far, back = (shift(value, **{axis: n}) for n in (1, 2, 3))
        value = (value + far) + (near + back)
    return value


def matmul_kernel(l0, l1, l2, l3, r0, r1, r2, r3, *outs):
    rows = outs[0].shape[0]
    for i, out in enumerate(outs):
        at = pl.ds(i * rows, rows)
        total = jnp.dot(l0[at, :], r0[...], preferred_element_type=F32)
        for left, right in ((l1, r1), (l2, r2), (l3, r3)):
            total += jnp.dot(left[at, :], right[...], preferred_element_type=F32)
        out[...] = total.astype(BF16)


def block_products(lefts, rights):
    rows, depth = lefts[0].shape
    width = rights[0].shape[1]
    tile = min(512, width)
    part = rows // 4
    return pl.pallas_call(
        matmul_kernel,
        grid=(width // tile,),
        in_specs=[pl.BlockSpec((rows, depth), lambda i: (0, 0))] * 4
        + [pl.BlockSpec((depth, tile), lambda i: (0, i))] * 4,
        out_specs=[pl.BlockSpec((part, tile), lambda i: (0, i))] * 4,
        out_shape=[jax.ShapeDtypeStruct((part, width), BF16)] * 4,
        compiler_params=pltpu.CompilerParams(vmem_limit_bytes=32 * 1024 * 1024),
        cost_estimate=pl.CostEstimate(
            flops=2 * rows * depth * 4 * width,
            bytes_accessed=2 * (4 * rows * depth + 4 * depth * width + rows * width),
            transcendentals=0,
        ),
    )(*lefts, *rights)


def per_device(inputs, grads_out, domain_weight, domain_ids, mix_weights):
    dom = lax.axis_index("dom")
    shard = lax.axis_index("shard")
    z, x_lo = dom // 2, dom % 2
    x_hi, y, core = shard // 8, (shard // 2) % 4, shard % 2
    count = D_IN * WIN
    hi = lax.Precision.HIGHEST
    weight = domain_weight[0]

    blocks = inputs.T.reshape(2, 4, 2, 256, 256)

    def columns_of(x_hi_to, core_to):
        mine = lax.dynamic_index_in_dim(blocks, x_hi_to, 0, keepdims=False)
        mine = lax.dynamic_index_in_dim(mine, core_to, 1, keepdims=False)
        turned = lax.dynamic_slice_in_dim(jnp.concatenate([mine, mine]), y, 4, 0)
        halves = turned.reshape(8, HALF, 256)
        return jnp.concatenate([halves[i] for i in (0, 1, 2, 7, 4, 3, 5, 6)])

    lefts = [
        columns_of(x_hi, core),
        shift(columns_of(x_hi, 1 - core), core=1),
        shift(columns_of(1 - x_hi, core), dx=2),
        shift(columns_of(1 - x_hi, 1 - core), dx=2, core=1),
    ]

    slots = []
    square = jnp.zeros((), F32)
    gram_slots = jnp.zeros((8, 8), F32)
    start = 0
    for width in CHUNKS:
        right = lax.slice_in_dim(grads_out, start, start + width, axis=1)
        across = shift(right, dx=2)
        rights = [right, shift(right, core=1), across, shift(across, core=1)]
        own, keep, up, down = block_products(lefts, rights)
        from_back = shift(up, dy=1)
        from_next = shift(down, dy=-1)
        back2 = shift((keep[:HALF].astype(F32) + from_back[:HALF].astype(F32)).astype(BF16), dy=1)
        next2 = shift((keep[HALF:].astype(F32) + from_next[:HALF].astype(F32)).astype(BF16), dy=-1)
        top = own[:HALF].astype(F32) + back2.astype(F32) + from_next[HALF:].astype(F32)
        bottom = own[HALF:].astype(F32) + from_back[HALF:].astype(F32) + next2.astype(F32)
        weff_grad = jnp.concatenate([top, bottom])
        center = (weff_grad * weight[:, start : start + width].astype(F32)).astype(BF16)
        square = square + jnp.sum(jnp.square(center.astype(F32)))
        halves = center.reshape(2, 4, 32, width)
        kept = lax.dynamic_index_in_dim(halves, x_lo, 0, keepdims=False)
        passed = shift(lax.dynamic_index_in_dim(halves, 1 - x_lo, 0, keepdims=False), pair=1)
        both = jnp.stack([kept, passed])
        parts = [
            lax.dynamic_index_in_dim(both, (z + n) % 4, 1, keepdims=False) for n in range(4)
        ]
        received = jnp.concatenate(
            [parts[0]] + [shift(parts[n], dz=n) for n in (1, 2, 3)]
        )
        flat = received.reshape(8, -1)
        gram_slots = gram_slots + lax.dot_general(
            flat, flat, (((1,), (1,)), ((), ())), preferred_element_type=F32
        )
        slots.append(received)
        start += width

    labels = jnp.arange(8, dtype=jnp.int32)
    group_of = ((z - labels // 2) % 4) * 2 + (x_lo ^ (labels % 2))
    place = (group_of[:, None] == labels[None, :]).astype(F32)
    onehot = (domain_ids[:, None] == labels[None, :]).astype(F32)

    mine = jnp.where(labels == dom, square, 0.0)
    diag = sum_everywhere(jnp.broadcast_to(mine[:, None], (8, 128)))[:, 0] / count
    weights = jnp.dot(onehot, mix_weights, precision=hi)
    scale = weights / jnp.sqrt(diag + 1e-06)
    slot_scale = jnp.dot(place, scale, precision=hi)
    owned = jnp.concatenate(
        [jnp.einsum("a,arc->rc", slot_scale, s.astype(F32), precision=hi).astype(BF16) for s in slots],
        axis=1,
    )

    pieces = [owned, shift(owned, pair=1)]
    for n in (1, 2, 3):
        pieces += [shift(owned, dz=n), shift(owned, dz=n, pair=1)]
    combined = jnp.zeros((256, WIN), BF16)
    for n in range(4):
        for b in range(2):
            row = (x_lo ^ b) * 128 + ((z - n) % 4) * 32
            combined = lax.dynamic_update_slice(combined, pieces[n * 2 + b], (row, 0))

    local = jnp.dot(jnp.dot(place.T, gram_slots, precision=hi), place, precision=hi)
    group_gram = sum_everywhere(local) / count
    gram = jnp.dot(jnp.dot(onehot.T, group_gram, precision=hi), onehot, precision=hi)
    return (combined, gram)


def solution(mesh):
    in_specs = (
        P(AXES, None),
        P(AXES, None),
        P("dom", "shard", None),
        P(),
        P(),
    )
    out_specs = (P("shard", None), P())
    return jax.shard_map(
        per_device, mesh=mesh, in_specs=in_specs, out_specs=out_specs, check_vma=False
    )
```

```python
import functools

import jax
import jax.numpy as jnp
from jax import lax
from jax.experimental import pallas as pl
from jax.experimental.pallas import tpu as pltpu
from jax.sharding import PartitionSpec as P

D_IN = 4096
WIN = 4096
AXES = ("dom", "shard")
EARLY = 1024
PIECES = ((1024,), (1024,), (512, 512))
HALF = 128
ORDER = ((0, 0), (0, 1), (1, 0), (3, 1), (2, 0), (1, 1), (2, 1), (3, 0))
PEERS = ((False, False), (False, True), (True, False), (True, True))
F32 = jnp.float32
BF16 = jnp.bfloat16


def device_index(x, y, z, core):
    return (z * 2 + x % 2) * 16 + (x // 2) * 8 + y * 2 + core


def shift(value, dx=0, dy=0, dz=0, pair=0, core=0):
    moves = [
        (
            device_index(x, y, z, c),
            device_index(((x ^ pair) + dx) % 4, (y + dy) % 4, (z + dz) % 4, c ^ core),
        )
        for x in range(4)
        for y in range(4)
        for z in range(4)
        for c in range(2)
    ]
    return lax.ppermute(value, AXES, moves)


def turn_kernel(at_ref, source, *outs):
    x_hi, y, core = at_ref[0], at_ref[1], at_ref[2]
    for out, (flip_x, flip_core) in zip(outs, PEERS):
        a = 1 - x_hi if flip_x else x_hi
        c = 1 - core if flip_core else core
        for i, (step, half) in enumerate(ORDER):
            block = ((a * 4 + lax.rem(y + step, 4)) * 2 + c) * 2 + half
            columns = pl.ds(pl.multiple_of(block * HALF, HALF), HALF)
            out[pl.ds(i * HALF, HALF), :] = source[:, columns].T


def turned_columns(inputs, at):
    rows = inputs.shape[0]
    return pl.pallas_call(
        turn_kernel,
        in_specs=[
            pl.BlockSpec(memory_space=pltpu.SMEM),
            pl.BlockSpec(memory_space=pltpu.VMEM),
        ],
        out_specs=[pl.BlockSpec(memory_space=pltpu.VMEM)] * 4,
        out_shape=[jax.ShapeDtypeStruct((8 * HALF, rows), BF16)] * 4,
        compiler_params=pltpu.CompilerParams(vmem_limit_bytes=16 * 1024 * 1024),
        cost_estimate=pl.CostEstimate(
            flops=0, bytes_accessed=4 * inputs.size, transcendentals=0
        ),
    )(at, inputs)


def matmul_kernel(sets, terms, *refs):
    lefts, rights, outs = refs[: sets * terms], refs[sets * terms : -4], refs[-4:]
    rows = outs[0].shape[1]
    for r in range(sets):
        for i, out in enumerate(outs):
            total = None
            for left, right in zip(lefts[r * terms : (r + 1) * terms], rights):
                term = jnp.dot(left[pl.ds(i * rows, rows), :], right[...], preferred_element_type=F32)
                total = term if total is None else total + term
            out[r] = total.astype(BF16)


def block_products(sets, rights, offsets, width):
    rows, depth = sets[0][0].shape
    terms = len(rights)
    tile = 512
    part = rows // 4

    def columns(offset):
        return pl.BlockSpec((depth, tile), lambda i: (0, i + offset // tile))

    n = len(sets)
    return pl.pallas_call(
        functools.partial(matmul_kernel, n, terms),
        grid=(width // tile,),
        in_specs=[pl.BlockSpec((rows, depth), lambda i: (0, 0))] * (n * terms)
        + [columns(offset) for offset in offsets],
        out_specs=[pl.BlockSpec((n, part, tile), lambda i: (0, 0, i))] * 4,
        out_shape=[jax.ShapeDtypeStruct((n, part, width), BF16)] * 4,
        compiler_params=pltpu.CompilerParams(vmem_limit_bytes=32 * 1024 * 1024),
        cost_estimate=pl.CostEstimate(
            flops=2 * n * rows * depth * terms * width,
            bytes_accessed=2 * (n * terms * rows * depth + terms * depth * width + n * rows * width),
            transcendentals=0,
        ),
    )(*sum(sets, []), *rights)


def after(values, *done):
    out = lax.optimization_barrier((tuple(values), done))
    return out[0]


def add(a, b):
    return (a.astype(F32) + b.astype(F32)).astype(BF16)


def per_device(inputs, grads_out, domain_weight, domain_ids, mix_weights):
    dom = lax.axis_index("dom")
    shard = lax.axis_index("shard")
    z, x_lo = dom // 2, dom % 2
    x_hi, y, core = shard // 8, (shard // 2) % 4, shard % 2
    count = D_IN * WIN
    hi = lax.Precision.HIGHEST
    weight = domain_weight[0]

    widths = [sum(piece) for piece in PIECES]
    edges = [EARLY + sum(widths[:p]) for p in range(len(widths) + 1)]
    own_left, core_left, x_left, both_left = turned_columns(inputs, jnp.stack([x_hi, y, core]))
    grads_core = shift(grads_out, core=1)
    lefts = [own_left, shift(core_left, core=1), shift(x_left, dx=2), shift(both_left, dx=2, core=1)]
    other_rows = [x_left, shift(both_left, core=1)]
    in_flight = [lefts[2], lefts[3]]
    across = []
    for lo, up in zip(edges, edges[1:]):
        (piece,) = after([lax.slice_in_dim(grads_out, lo, up, axis=1)], in_flight[-2])
        across.append(shift(piece, dx=2))
        in_flight.append(across[-1])
    swapped = [shift(a, core=1) for a in across]

    def reduce_first(products):
        own, keep, up, down = products
        return own, keep, shift(up, dy=1), shift(down, dy=-1)

    def reduce_second(first):
        own, keep, from_back, from_next = first
        sums = add(keep[:, :HALF], from_back[:, :HALF]), add(keep[:, HALF:], from_next[:, :HALF])
        return sums, (
            own, from_back[:, HALF:], from_next[:, HALF:], shift(sums[0], dy=1), shift(sums[1], dy=-1),
        )

    def reduce_last(second, *done):
        own, back_own, next_own, back2, next2 = after(second, *done)
        top = own[:, :HALF].astype(F32) + back2.astype(F32) + next_own.astype(F32)
        bottom = own[:, HALF:].astype(F32) + back_own.astype(F32) + next2.astype(F32)
        return jnp.concatenate([top, bottom], axis=1)

    def centered(weff_grad, start):
        block = weight[:, start : start + weff_grad.shape[1]].astype(F32)
        return (weff_grad * block).astype(BF16)

    def spread_x(*centers):
        pairs = jnp.concatenate(centers, axis=1).reshape(4, 2, 32, -1)
        kept = lax.dynamic_index_in_dim(pairs, x_lo, 1, keepdims=False)
        return kept, shift(lax.dynamic_index_in_dim(pairs, 1 - x_lo, 1, keepdims=False), pair=1)

    def spread_z(kept, passed):
        both = jnp.stack([kept, passed])
        parts = [lax.dynamic_index_in_dim(both, (z + n) % 4, 1, keepdims=False) for n in range(4)]
        return jnp.concatenate([parts[0]] + [shift(parts[n], dz=n) for n in (1, 2, 3)])

    def products(p, inner, width, *done):
        rights = after([across[p], swapped[p]], *done)
        start = edges[p] + inner
        return block_products([lefts], [grads_out, grads_core, *rights], [start, start, inner, inner], width)

    early = reduce_first(
        block_products([lefts[:2], other_rows], [grads_out, grads_core], [0, 0], EARLY)
    )
    early_sums, early = reduce_second(early)

    out1 = products(0, 0, 1024, *early_sums)
    first1 = reduce_first(out1)
    early = reduce_last(early, out1[2])
    early_other = shift(early[1].astype(BF16), dx=2)
    sums1, second1 = reduce_second(first1)

    out2 = products(1, 0, 1024, *sums1)
    first2 = reduce_first(out2)
    center1 = centered(reduce_last(second1, out2[2])[0], edges[0])
    center0 = centered(early[0] + early_other.astype(F32), 0)
    half_a = spread_x(center0, center1)
    sums2, second2 = reduce_second(first2)

    out3 = products(2, 0, 512, *sums2, center0, center1)
    first3 = reduce_first(out3)
    slots_a = spread_z(*after(half_a, out3[2]))
    sums3, second3 = reduce_second(first3)

    out4 = products(2, 512, 512, *sums3)
    first4 = reduce_first(out4)
    center2 = centered(reduce_last(second2, out4[2])[0], edges[1])
    sums4, second4 = reduce_second(first4)
    center3 = centered(reduce_last(second3, *sums4)[0], edges[2])
    slots_b = spread_z(*spread_x(center2, center3))
    center4 = centered(reduce_last(second4)[0], edges[2] + 512)
    slots_c = lax.all_to_all(center4.reshape(8, 32, -1), "dom", 0, 0, tiled=True)

    labels = jnp.arange(8, dtype=jnp.int32)
    group_of = ((z - labels // 2) % 4) * 2 + (x_lo ^ (labels % 2))
    place = (group_of[:, None] == labels[None, :]).astype(F32)
    onehot = (domain_ids[:, None] == labels[None, :]).astype(F32)
    weights = jnp.dot(onehot, mix_weights, precision=hi)

    def partial_gram(slots):
        flat = slots.reshape(8, -1)
        return lax.dot_general(flat, flat, (((1,), (1,)), ((), ())), preferred_element_type=F32)

    placed = partial_gram(slots_a) + partial_gram(slots_b)
    placed = jnp.sum(
        place[:, :, None, None] * place[None, None] * placed[:, None, :, None], axis=(0, 2)
    )
    local = placed + partial_gram(slots_c)
    sent = jnp.broadcast_to(jnp.pad(local, ((0, 0), (0, 120)))[None], (128, 8, 128))
    parts = lax.all_to_all(sent, AXES, 0, 0, tiled=True)
    group_gram = jnp.sum(parts, axis=0)[:, :8] / count
    scale = weights / jnp.sqrt(jnp.diagonal(group_gram) + 1e-06)
    slot_scale = jnp.dot(place, scale, precision=hi)

    def mixed(factors, slots):
        return jnp.sum(factors[:, None, None] * slots.astype(F32), axis=0).astype(BF16)

    owned = jnp.concatenate(
        [mixed(slot_scale, slots_a), mixed(slot_scale, slots_b), mixed(scale, slots_c)], axis=1
    )
    combined = lax.all_to_all(jnp.broadcast_to(owned[None], (8, *owned.shape)), "dom", 0, 0, tiled=True)
    gram = jnp.dot(jnp.dot(onehot.T, group_gram, precision=hi), onehot, precision=hi)
    return (combined.reshape(-1, WIN), gram)


def solution(mesh):
    in_specs = (
        P(AXES, None),
        P(AXES, None),
        P("dom", "shard", None),
        P(),
        P(),
    )
    out_specs = (P("shard", None), P())
    return jax.shard_map(
        per_device, mesh=mesh, in_specs=in_specs, out_specs=out_specs, check_vma=False
    )
```

```python
import functools

import jax
import jax.numpy as jnp
from jax import lax
from jax.experimental import pallas as pl
from jax.experimental.pallas import tpu as pltpu
from jax.sharding import PartitionSpec as P

D_IN = 4096
WIN = 4096
AXES = ("dom", "shard")
EARLY = 1024
CHUNKS = (1024, 1024, 1024)
PIECES = ((0,), (1, 2))
HALF = 128
ORDER = ((0, 0), (0, 1), (1, 0), (3, 1), (2, 0), (1, 1), (2, 1), (3, 0))
PEERS = ((False, False), (False, True), (True, False), (True, True))
F32 = jnp.float32
BF16 = jnp.bfloat16


def device_index(x, y, z, core):
    return (z * 2 + x % 2) * 16 + (x // 2) * 8 + y * 2 + core


def shift(value, dx=0, dy=0, dz=0, pair=0, core=0):
    moves = [
        (
            device_index(x, y, z, c),
            device_index(((x ^ pair) + dx) % 4, (y + dy) % 4, (z + dz) % 4, c ^ core),
        )
        for x in range(4)
        for y in range(4)
        for z in range(4)
        for c in range(2)
    ]
    return lax.ppermute(value, AXES, moves)


def turn_kernel(at_ref, source, *outs):
    x_hi, y, core = at_ref[0], at_ref[1], at_ref[2]
    depth = source.shape[0]
    for out, (flip_x, flip_core) in zip(outs, PEERS):
        a = 1 - x_hi if flip_x else x_hi
        c = 1 - core if flip_core else core
        for i, (step, half) in enumerate(ORDER):
            block = ((a * 4 + lax.rem(y + step, 4)) * 2 + c) * 2 + half
            columns = pl.ds(pl.multiple_of(block * HALF, HALF), HALF)
            out[pl.ds(i % 2 * HALF, HALF), pl.ds(i // 2 * depth, depth)] = source[:, columns].T


def turned_columns(inputs, at):
    rows = inputs.shape[0]
    return pl.pallas_call(
        turn_kernel,
        in_specs=[
            pl.BlockSpec(memory_space=pltpu.SMEM),
            pl.BlockSpec(memory_space=pltpu.VMEM),
        ],
        out_specs=[pl.BlockSpec(memory_space=pltpu.VMEM)] * 4,
        out_shape=[jax.ShapeDtypeStruct((2 * HALF, 4 * rows), BF16)] * 4,
        compiler_params=pltpu.CompilerParams(vmem_limit_bytes=16 * 1024 * 1024),
        cost_estimate=pl.CostEstimate(
            flops=0, bytes_accessed=4 * inputs.size, transcendentals=0
        ),
    )(at, inputs)


def matmul_kernel(sets, terms, *refs):
    lefts, rights, outs = refs[: sets * terms], refs[sets * terms : -4], refs[-4:]
    depth = rights[0].shape[0]
    for r in range(sets):
        for i, out in enumerate(outs):
            total = None
            for left, right in zip(lefts[r * terms : (r + 1) * terms], rights):
                term = jnp.dot(
                    left[:, pl.ds(i * depth, depth)], right[...], preferred_element_type=F32
                )
                total = term if total is None else total + term
            out[r] = total.astype(BF16)


def block_products(sets, rights, width):
    rows, depth = 2 * HALF, rights[0][0].shape[0]
    tile = 512
    n, terms = len(sets), len(rights)
    lefts = sum(sets, [])

    def left_spec(offset):
        return pl.BlockSpec((rows, 4 * depth), lambda i: (0, offset // (4 * depth)))

    def right_spec(offset):
        return pl.BlockSpec((depth, tile), lambda i: (0, i + offset // tile))

    return pl.pallas_call(
        functools.partial(matmul_kernel, n, terms),
        grid=(width // tile,),
        in_specs=[left_spec(o) for _, o in lefts] + [right_spec(o) for _, o in rights],
        out_specs=[pl.BlockSpec((n, rows, tile), lambda i: (0, 0, i))] * 4,
        out_shape=[jax.ShapeDtypeStruct((n, rows, width), BF16)] * 4,
        compiler_params=pltpu.CompilerParams(vmem_limit_bytes=32 * 1024 * 1024),
        cost_estimate=pl.CostEstimate(
            flops=0, bytes_accessed=0,
            transcendentals=0,
        ),
    )(*[v for v, _ in lefts], *[v for v, _ in rights])


def after(values, *done):
    out = lax.optimization_barrier((tuple(values), done))
    return out[0]


def add(a, b):
    return (a.astype(F32) + b.astype(F32)).astype(BF16)


def per_device(inputs, grads_out, domain_weight, domain_ids, mix_weights):
    dom = lax.axis_index("dom")
    shard = lax.axis_index("shard")
    x_hi, y, core = shard // 8, (shard // 2) % 4, shard % 2
    count = D_IN * WIN
    hi = lax.Precision.HIGHEST
    weight = domain_weight[0]

    n_chunks = len(CHUNKS)
    starts = [EARLY + sum(CHUNKS[:k]) for k in range(n_chunks)]
    ends = [start + width for start, width in zip(starts, CHUNKS)]
    spans = [(starts[piece[0]], ends[piece[-1]]) for piece in PIECES]
    own_left, core_left, x_left, both_left = turned_columns(inputs, jnp.stack([x_hi, y, core]))
    grads_core = shift(grads_out, core=1)
    core_left = shift(core_left, core=1)
    both_left = shift(both_left, core=1)
    own_set = [(own_left, 0), (core_left, 0)]
    other_set = [(x_left, 0), (both_left, 0)]
    sent = jnp.concatenate([x_left, both_left, grads_out[:, slice(*spans[0])]], axis=1)
    skip = 2 * x_left.shape[1]
    across = [shift(sent, dx=2)]
    lefts = own_set + [(across[0], 0), (across[0], skip // 2)]
    waits = [sent, across[0]]
    for p in range(1, len(PIECES)):
        (piece,) = after([grads_out[:, slice(*spans[p])]], waits[p - 1])
        across.append(shift(piece, dx=2))
        waits.append(across[-1])
    def reduce_first(products):
        own, keep, up, down = products
        return own, keep, shift(up, dy=1), shift(down, dy=-1)

    def reduce_second(first):
        own, keep, from_back, from_next = first
        sums = add(keep[:, :HALF], from_back[:, :HALF]), add(keep[:, HALF:], from_next[:, :HALF])
        return sums, (
            own, from_back[:, HALF:], from_next[:, HALF:], shift(sums[0], dy=1), shift(sums[1], dy=-1),
        )

    def reduce_last(second, *done):
        own, back_own, next_own, back2, next2 = after(second, *done)
        top = own[:, :HALF].astype(F32) + back2.astype(F32) + next_own.astype(F32)
        bottom = own[:, HALF:].astype(F32) + back_own.astype(F32) + next2.astype(F32)
        return jnp.concatenate([top, bottom], axis=1)

    def centered(weff_grad, start):
        block = weight[:, start : start + weff_grad.shape[1]].astype(F32)
        return (weff_grad * block).astype(BF16)

    def spread(*centers):
        pieces = jnp.concatenate(centers, axis=1)
        return lax.all_to_all(pieces.reshape(8, 32, -1), "dom", 0, 0, tiled=True)

    swapped = {}

    def products(k, *done):
        p = next(p for p, piece in enumerate(PIECES) if k in piece)
        inner = starts[k] - spans[p][0]
        if p not in swapped:
            (far,) = after([across[p]], *done)
            swapped[p] = shift(far if p else far[:, skip:], core=1)
        far, far_core = after([across[p], swapped[p]], *done)
        rights = [
            (grads_out, starts[k]), (grads_core, starts[k]), (far, inner + (0 if p else skip)), (far_core, inner),
        ]
        return block_products([lefts], rights, CHUNKS[k])

    first = reduce_first(block_products([own_set, other_set], [(grads_out, 0), (grads_core, 0)], EARLY))
    sums, early = reduce_second(first)

    def partial_gram(slots):
        flat = slots.reshape(8, -1)
        return lax.dot_general(flat, flat, (((1,), (1,)), ((), ())), preferred_element_type=F32)

    out0 = products(0, *sums)
    first = reduce_first(out0)
    early = reduce_last(early, out0[2])
    early_other = early[1].astype(BF16)
    sums, second0 = reduce_second(first)
    out1 = products(1, *sums, early_other)
    early_other = shift(early_other, dx=2)
    first1 = reduce_first(out1)
    out2 = products(2, out1[2])
    first2 = reduce_first(out2)
    sums, second1 = reduce_second(after(first1, out2[2]))
    center_early = centered(early[0] + after([early_other], *sums)[0].astype(F32), 0)
    center0 = centered(reduce_last(second0, *sums)[0], starts[0])
    slots = [spread(center_early, center0)]
    sums, second2 = reduce_second(after(first2, center_early, center0))
    center1 = centered(reduce_last(second1, *sums)[0], starts[1])
    slots.append(spread(after([center1], slots[0])[0]))
    gram_slots = partial_gram(slots[0])
    center2 = centered(reduce_last(second2, center1, gram_slots, slots[1])[0], starts[2])
    slots.append(spread(center2))
    gram_slots = gram_slots + partial_gram(slots[1]) + partial_gram(slots[2])

    labels = jnp.arange(8, dtype=jnp.int32)
    onehot = (domain_ids[:, None] == labels[None, :]).astype(F32)
    weights = jnp.dot(onehot, mix_weights, precision=hi)

    local = gram_slots.reshape(1, 1, 64)
    sent = jnp.broadcast_to(jnp.pad(local, ((0, 0), (0, 0), (0, 64))), (128, 1, 128))
    parts = lax.all_to_all(sent, AXES, 0, 0, tiled=True)
    group_gram = jnp.sum(parts, axis=(0, 1))[:64].reshape(8, 8) / count
    scale = weights / jnp.sqrt(jnp.diagonal(group_gram) + 1e-06)

    def mixed(slots):
        return jnp.sum(scale[:, None, None] * slots.astype(F32), axis=0).astype(BF16)

    owned = jnp.concatenate([mixed(received) for received in slots], axis=1)
    combined = lax.all_to_all(jnp.broadcast_to(owned[None], (8, *owned.shape)), "dom", 0, 0, tiled=True)
    gram = jnp.dot(jnp.dot(onehot.T, group_gram, precision=hi), onehot, precision=hi)
    return (combined.reshape(-1, WIN), gram)


def solution(mesh):
    in_specs = (
        P(AXES, None),
        P(AXES, None),
        P("dom", "shard", None),
        P(),
        P(),
    )
    out_specs = (P("shard", None), P())
    return jax.shard_map(
        per_device, mesh=mesh, in_specs=in_specs, out_specs=out_specs, check_vma=False
    )
```

```python
import functools

import jax
import jax.numpy as jnp
from jax import lax
from jax.experimental import pallas as pl
from jax.experimental.pallas import tpu as pltpu
from jax.sharding import PartitionSpec as P

D_IN = 4096
WIN = 4096
AXES = ("dom", "shard")
EARLY = 1536
CHUNKS = (1024, 1536)
PIECES = ((0,), (1,))
HALF = 128
ORDER = ((0, 0), (0, 1), (1, 0), (3, 1), (2, 0), (1, 1), (2, 1), (3, 0))
PEERS = ((False, False), (False, True), (True, False), (True, True))
F32 = jnp.float32
BF16 = jnp.bfloat16


def device_index(x, y, z, core):
    return (z * 2 + x % 2) * 16 + (x // 2) * 8 + y * 2 + core


def shift(value, dx=0, dy=0, dz=0, pair=0, core=0):
    moves = [
        (
            device_index(x, y, z, c),
            device_index(((x ^ pair) + dx) % 4, (y + dy) % 4, (z + dz) % 4, c ^ core),
        )
        for x in range(4)
        for y in range(4)
        for z in range(4)
        for c in range(2)
    ]
    return lax.ppermute(value, AXES, moves)


def turn_kernel(at_ref, source, *outs):
    x_hi, y, core = at_ref[0], at_ref[1], at_ref[2]
    depth = source.shape[0]
    for out, (flip_x, flip_core) in zip(outs, PEERS):
        a = 1 - x_hi if flip_x else x_hi
        c = 1 - core if flip_core else core
        for i, (step, half) in enumerate(ORDER):
            block = ((a * 4 + lax.rem(y + step, 4)) * 2 + c) * 2 + half
            columns = pl.ds(pl.multiple_of(block * HALF, HALF), HALF)
            out[pl.ds(i % 2 * HALF, HALF), pl.ds(i // 2 * depth, depth)] = source[:, columns].T


def turned_columns(inputs, at):
    rows = inputs.shape[0]
    return pl.pallas_call(
        turn_kernel,
        in_specs=[
            pl.BlockSpec(memory_space=pltpu.SMEM),
            pl.BlockSpec(memory_space=pltpu.VMEM),
        ],
        out_specs=[pl.BlockSpec(memory_space=pltpu.VMEM)] * 4,
        out_shape=[jax.ShapeDtypeStruct((2 * HALF, 4 * rows), BF16)] * 4,
        compiler_params=pltpu.CompilerParams(vmem_limit_bytes=16 * 1024 * 1024),
        cost_estimate=pl.CostEstimate(
            flops=0, bytes_accessed=4 * inputs.size, transcendentals=0
        ),
    )(at, inputs)


def matmul_kernel(sets, terms, *refs):
    lefts, rights, outs = refs[: sets * terms], refs[sets * terms : -4], refs[-4:]
    depth = rights[0].shape[0]
    for r in range(sets):
        for i, out in enumerate(outs):
            total = None
            for left, right in zip(lefts[r * terms : (r + 1) * terms], rights):
                term = jnp.dot(
                    left[:, pl.ds(i * depth, depth)], right[...], preferred_element_type=F32
                )
                total = term if total is None else total + term
            out[r] = total.astype(BF16)


def block_products(sets, rights, width):
    rows, depth = 2 * HALF, rights[0][0].shape[0]
    tile = 512
    n, terms = len(sets), len(rights)
    lefts = sum(sets, [])

    def left_spec(offset):
        return pl.BlockSpec((rows, 4 * depth), lambda i: (0, offset // (4 * depth)))

    def right_spec(offset):
        return pl.BlockSpec((depth, tile), lambda i: (0, i + offset // tile))

    return pl.pallas_call(
        functools.partial(matmul_kernel, n, terms),
        grid=(width // tile,),
        in_specs=[left_spec(o) for _, o in lefts] + [right_spec(o) for _, o in rights],
        out_specs=[pl.BlockSpec((n, rows, tile), lambda i: (0, 0, i))] * 4,
        out_shape=[jax.ShapeDtypeStruct((n, rows, width), BF16)] * 4,
        compiler_params=pltpu.CompilerParams(vmem_limit_bytes=32 * 1024 * 1024),
        cost_estimate=pl.CostEstimate(
            flops=0, bytes_accessed=0,
            transcendentals=0,
        ),
    )(*[v for v, _ in lefts], *[v for v, _ in rights])


def after(values, *done):
    out = lax.optimization_barrier((tuple(values), done))
    return out[0]


def add(a, b):
    return (a.astype(F32) + b.astype(F32)).astype(BF16)


def per_device(inputs, grads_out, domain_weight, domain_ids, mix_weights):
    dom = lax.axis_index("dom")
    shard = lax.axis_index("shard")
    x_hi, y, core = shard // 8, (shard // 2) % 4, shard % 2
    count = D_IN * WIN
    hi = lax.Precision.HIGHEST
    weight = domain_weight[0]

    n_chunks = len(CHUNKS)
    starts = [EARLY + sum(CHUNKS[:k]) for k in range(n_chunks)]
    ends = [start + width for start, width in zip(starts, CHUNKS)]
    spans = [(starts[piece[0]], ends[piece[-1]]) for piece in PIECES]
    own_left, core_left, x_left, both_left = turned_columns(inputs, jnp.stack([x_hi, y, core]))
    grads_core = shift(grads_out, core=1)
    core_left = shift(core_left, core=1)
    both_left = shift(both_left, core=1)
    own_set = [(own_left, 0), (core_left, 0)]
    other_set = [(x_left, 0), (both_left, 0)]
    sent = jnp.concatenate([x_left, both_left, grads_out[:, slice(*spans[0])]], axis=1)
    skip = 2 * x_left.shape[1]
    across = [shift(sent, dx=2)]
    lefts = own_set + [(across[0], 0), (across[0], skip // 2)]
    waits = [sent, across[0]]
    for p in range(1, len(PIECES)):
        (piece,) = after([grads_out[:, slice(*spans[p])]], waits[p - 1])
        across.append(shift(piece, dx=2))
        waits.append(across[-1])
    def reduce_first(products):
        own, keep, up, down = products
        return own, keep, shift(up, dy=1), shift(down, dy=-1)

    def reduce_second(first):
        own, keep, from_back, from_next = first
        sums = add(keep[:, :HALF], from_back[:, :HALF]), add(keep[:, HALF:], from_next[:, :HALF])
        return sums, (
            own, from_back[:, HALF:], from_next[:, HALF:], shift(sums[0], dy=1), shift(sums[1], dy=-1),
        )

    def reduce_last(second, *done):
        own, back_own, next_own, back2, next2 = after(second, *done)
        top = own[:, :HALF].astype(F32) + back2.astype(F32) + next_own.astype(F32)
        bottom = own[:, HALF:].astype(F32) + back_own.astype(F32) + next2.astype(F32)
        return jnp.concatenate([top, bottom], axis=1)

    def centered(weff_grad, start):
        block = weight[:, start : start + weff_grad.shape[1]].astype(F32)
        return (weff_grad * block).astype(BF16)

    def spread(*centers):
        pieces = jnp.concatenate(centers, axis=1)
        return lax.all_to_all(pieces.reshape(8, 32, -1), "dom", 0, 0, tiled=True)

    swapped = {}

    def products(k, *done):
        p = next(p for p, piece in enumerate(PIECES) if k in piece)
        inner = starts[k] - spans[p][0]
        if p not in swapped:
            (far,) = after([across[p]], *done)
            swapped[p] = shift(far if p else far[:, skip:], core=1)
        far, far_core = after([across[p], swapped[p]], *done)
        rights = [
            (grads_out, starts[k]), (grads_core, starts[k]), (far, inner + (0 if p else skip)), (far_core, inner),
        ]
        return block_products([lefts], rights, CHUNKS[k])

    first = reduce_first(block_products([own_set, other_set], [(grads_out, 0), (grads_core, 0)], EARLY))
    sums, early = reduce_second(first)

    def partial_gram(slots):
        flat = slots.reshape(8, -1)
        return lax.dot_general(flat, flat, (((1,), (1,)), ((), ())), preferred_element_type=F32)

    out0 = products(0, *sums)
    first0 = reduce_first(out0)
    out1 = products(1, out0[2], *early)
    first1 = reduce_first(out1)
    early = reduce_last(early, out1[2])
    early_other = shift(early[1].astype(BF16), dx=2)
    sums, second0 = reduce_second(after(first0, out1[2]))
    sums, second1 = reduce_second(after(first1, *sums))
    center_early = centered(early[0] + after([early_other], *sums)[0].astype(F32), 0)
    slots = [spread(center_early)]
    center0 = centered(reduce_last(second0, center_early)[0], starts[0])
    center1 = centered(reduce_last(second1, center0)[0], starts[1])
    slots.append(spread(after([center0], slots[0])[0], center1))
    gram_slots = partial_gram(after([slots[0]], center1)[0]) + partial_gram(slots[1])

    labels = jnp.arange(8, dtype=jnp.int32)
    onehot = (domain_ids[:, None] == labels[None, :]).astype(F32)
    weights = jnp.dot(onehot, mix_weights, precision=hi)

    local = gram_slots.reshape(1, 1, 64)
    sent = jnp.broadcast_to(jnp.pad(local, ((0, 0), (0, 0), (0, 64))), (128, 1, 128))
    parts = lax.all_to_all(sent, AXES, 0, 0, tiled=True)
    group_gram = jnp.sum(parts, axis=(0, 1))[:64].reshape(8, 8) / count
    scale = weights / jnp.sqrt(jnp.diagonal(group_gram) + 1e-06)

    def mixed(slots):
        return jnp.sum(scale[:, None, None] * slots.astype(F32), axis=0).astype(BF16)

    owned = jnp.concatenate([mixed(received) for received in slots], axis=1)
    combined = lax.all_to_all(jnp.broadcast_to(owned[None], (8, *owned.shape)), "dom", 0, 0, tiled=True)
    gram = jnp.dot(jnp.dot(onehot.T, group_gram, precision=hi), onehot, precision=hi)
    return (combined.reshape(-1, WIN), gram)


def solution(mesh):
    in_specs = (
        P(AXES, None),
        P(AXES, None),
        P("dom", "shard", None),
        P(),
        P(),
    )
    out_specs = (P("shard", None), P())
    return jax.shard_map(
        per_device, mesh=mesh, in_specs=in_specs, out_specs=out_specs, check_vma=False
    )
```

```python
import functools

import jax
import jax.numpy as jnp
from jax import lax
from jax.experimental import pallas as pl
from jax.experimental.pallas import tpu as pltpu
from jax.sharding import PartitionSpec as P

D_IN = 4096
WIN = 4096
AXES = ("dom", "shard")
EARLY = 1536
CHUNKS = (1024, 1536)
PIECES = ((0,), (1,))
HALF = 128
ORDER = ((0, 0), (0, 1), (1, 0), (3, 1), (2, 0), (1, 1), (2, 1), (3, 0))
PEERS = ((False, False), (False, True), (True, False), (True, True))
F32 = jnp.float32
BF16 = jnp.bfloat16


def device_index(x, y, z, core):
    return (z * 2 + x % 2) * 16 + (x // 2) * 8 + y * 2 + core


def shift(value, dx=0, dy=0, dz=0, pair=0, core=0):
    moves = [
        (
            device_index(x, y, z, c),
            device_index(((x ^ pair) + dx) % 4, (y + dy) % 4, (z + dz) % 4, c ^ core),
        )
        for x in range(4)
        for y in range(4)
        for z in range(4)
        for c in range(2)
    ]
    return lax.ppermute(value, AXES, moves)


def turn_kernel(at_ref, source, *outs):
    x_hi, y, core = at_ref[0], at_ref[1], at_ref[2]
    depth = source.shape[0]
    for out, (flip_x, flip_core) in zip(outs, PEERS):
        a = 1 - x_hi if flip_x else x_hi
        c = 1 - core if flip_core else core
        for i, (step, half) in enumerate(ORDER):
            block = ((a * 4 + lax.rem(y + step, 4)) * 2 + c) * 2 + half
            columns = pl.ds(pl.multiple_of(block * HALF, HALF), HALF)
            out[pl.ds(i % 2 * HALF, HALF), pl.ds(i // 2 * depth, depth)] = source[:, columns].T


def turned_columns(inputs, at):
    rows = inputs.shape[0]
    return pl.pallas_call(
        turn_kernel,
        in_specs=[
            pl.BlockSpec(memory_space=pltpu.SMEM),
            pl.BlockSpec(memory_space=pltpu.VMEM),
        ],
        out_specs=[pl.BlockSpec(memory_space=pltpu.VMEM)] * 4,
        out_shape=[jax.ShapeDtypeStruct((2 * HALF, 4 * rows), BF16)] * 4,
        compiler_params=pltpu.CompilerParams(vmem_limit_bytes=16 * 1024 * 1024),
        cost_estimate=pl.CostEstimate(
            flops=0, bytes_accessed=4 * inputs.size, transcendentals=0
        ),
    )(at, inputs)


def matmul_kernel(sets, terms, *refs):
    lefts, rights, outs = refs[: sets * terms], refs[sets * terms : -4], refs[-4:]
    depth = rights[0].shape[0]
    for r in range(sets):
        for i, out in enumerate(outs):
            total = None
            for left, right in zip(lefts[r * terms : (r + 1) * terms], rights):
                term = jnp.dot(
                    left[:, pl.ds(i * depth, depth)], right[...], preferred_element_type=F32
                )
                total = term if total is None else total + term
            out[r] = total.astype(BF16)


def block_products(sets, rights, width):
    rows, depth = 2 * HALF, rights[0][0].shape[0]
    tile = 512
    n, terms = len(sets), len(rights)
    lefts = sum(sets, [])

    def left_spec(offset):
        return pl.BlockSpec((rows, 4 * depth), lambda i: (0, offset // (4 * depth)))

    def right_spec(offset):
        return pl.BlockSpec((depth, tile), lambda i: (0, i + offset // tile))

    return pl.pallas_call(
        functools.partial(matmul_kernel, n, terms),
        grid=(width // tile,),
        in_specs=[left_spec(o) for _, o in lefts] + [right_spec(o) for _, o in rights],
        out_specs=[pl.BlockSpec((n, rows, tile), lambda i: (0, 0, i))] * 4,
        out_shape=[jax.ShapeDtypeStruct((n, rows, width), BF16)] * 4,
        compiler_params=pltpu.CompilerParams(vmem_limit_bytes=32 * 1024 * 1024),
        cost_estimate=pl.CostEstimate(
            flops=0, bytes_accessed=0,
            transcendentals=0,
        ),
    )(*[v for v, _ in lefts], *[v for v, _ in rights])


def after(values, *done):
    out = lax.optimization_barrier((tuple(values), done))
    return out[0]


def finish_kernel(offset, ready, own, from_back, from_next, back2, next2, weight, out):
    before, width = ready.shape[1], own.shape[2]
    out[:, pl.ds(0, before)] = ready[...]
    for half, first, second in ((0, from_next, back2), (1, from_back, next2)):
        rows = pl.ds(half * HALF, HALF)
        total = own[0, rows, :].astype(F32) + second[0].astype(F32)
        total += first[0, pl.ds(HALF, HALF), :].astype(F32)
        scaled = total * weight[rows, pl.ds(offset, width)].astype(F32)
        out[rows, pl.ds(before, width)] = scaled.astype(BF16)


def finished(ready, second, weight, offset):
    whole = pl.BlockSpec(memory_space=pltpu.VMEM)
    width = ready.shape[1] + second[0].shape[2]
    return pl.pallas_call(
        functools.partial(finish_kernel, offset),
        in_specs=[whole] * 7,
        out_specs=whole,
        out_shape=jax.ShapeDtypeStruct((2 * HALF, width), BF16),
        compiler_params=pltpu.CompilerParams(vmem_limit_bytes=40 * 1024 * 1024),
        cost_estimate=pl.CostEstimate(flops=0, bytes_accessed=0, transcendentals=0),
    )(ready, *second, weight)


def add(a, b):
    return (a.astype(F32) + b.astype(F32)).astype(BF16)


def per_device(inputs, grads_out, domain_weight, domain_ids, mix_weights):
    dom = lax.axis_index("dom")
    shard = lax.axis_index("shard")
    z, x_lo = dom // 2, dom % 2
    x_hi, y, core = shard // 8, (shard // 2) % 4, shard % 2
    count = D_IN * WIN
    hi = lax.Precision.HIGHEST
    weight = domain_weight[0]

    n_chunks = len(CHUNKS)
    starts = [EARLY + sum(CHUNKS[:k]) for k in range(n_chunks)]
    ends = [start + width for start, width in zip(starts, CHUNKS)]
    spans = [(starts[piece[0]], ends[piece[-1]]) for piece in PIECES]
    own_left, core_left, x_left, both_left = turned_columns(inputs, jnp.stack([x_hi, y, core]))
    grads_core = shift(grads_out, core=1)
    core_left = shift(core_left, core=1)
    both_left = shift(both_left, core=1)
    own_set = [(own_left, 0), (core_left, 0)]
    other_set = [(x_left, 0), (both_left, 0)]
    sent = jnp.concatenate([x_left, both_left, grads_out[:, slice(*spans[0])]], axis=1)
    skip = 2 * x_left.shape[1]
    across = [shift(sent, dx=2)]
    lefts = own_set + [(across[0], 0), (across[0], skip // 2)]
    waits = [sent, across[0]]
    for p in range(1, len(PIECES)):
        (piece,) = after([grads_out[:, slice(*spans[p])]], waits[p - 1])
        across.append(shift(piece, dx=2))
        waits.append(across[-1])
    def reduce_first(products):
        own, keep, up, down = products
        return own, keep, shift(up, dy=1), shift(down, dy=-1)

    def reduce_second(first):
        own, keep, from_back, from_next = first
        sums = add(keep[:, :HALF], from_back[:, :HALF]), add(keep[:, HALF:], from_next[:, :HALF])
        return sums, (
            own, from_back, from_next, shift(sums[0], dy=1), shift(sums[1], dy=-1),
        )

    def reduce_last(second, *done):
        own, from_back, from_next, back2, next2 = after(second, *done)
        top = own[:, :HALF].astype(F32) + back2.astype(F32) + from_next[:, HALF:].astype(F32)
        bottom = own[:, HALF:].astype(F32) + from_back[:, HALF:].astype(F32) + next2.astype(F32)
        return jnp.concatenate([top, bottom], axis=1)

    def centered(weff_grad, start):
        block = weight[:, start : start + weff_grad.shape[1]].astype(F32)
        return (weff_grad * block).astype(BF16)

    def spread(*centers):
        pieces = jnp.concatenate(centers, axis=1)
        return lax.all_to_all(pieces.reshape(8, 32, -1), "dom", 0, 0, tiled=True)

    swapped = {}

    def products(k, *done, swap_after=()):
        p = next(p for p, piece in enumerate(PIECES) if k in piece)
        inner = starts[k] - spans[p][0]
        if p not in swapped:
            (far,) = after([across[p]], *(swap_after or done))
            swapped[p] = shift(far if p else far[:, skip:], core=1)
        far, far_core = after([across[p], swapped[p]], *done)
        rights = [
            (grads_out, starts[k]), (grads_core, starts[k]), (far, inner + (0 if p else skip)), (far_core, inner),
        ]
        return block_products([lefts], rights, CHUNKS[k])

    first = reduce_first(block_products([own_set, other_set], [(grads_out, 0), (grads_core, 0)], EARLY))
    sums, early = reduce_second(first)

    def partial_gram(slots):
        flat = slots.reshape(8, -1)
        return lax.dot_general(flat, flat, (((1,), (1,)), ((), ())), preferred_element_type=F32)

    out0 = products(0, *sums)
    first0 = reduce_first(out0)
    out1 = products(1, out0[2], *early, swap_after=out0[2:3])
    early = reduce_last(early, out0[2])
    early_other = shift(early[1].astype(BF16), dx=2)
    first1 = reduce_first(out1)
    sums, second0 = reduce_second(after(first0, out1[2]))
    center_early = centered(early[0] + after([early_other], *sums)[0].astype(F32), 0)
    slots = [spread(center_early)]
    sums, second1 = reduce_second(after(first1, center_early))
    center0 = centered(reduce_last(second0, *sums)[0], starts[0])
    center = finished(center0, second1, weight, starts[1])
    slots.append(spread(after([center], slots[0])[0]))
    gram_slots = partial_gram(after([slots[0]], center)[0]) + partial_gram(slots[1])

    labels = jnp.arange(8, dtype=jnp.int32)
    onehot = (domain_ids[:, None] == labels[None, :]).astype(F32)
    weights = jnp.dot(onehot, mix_weights, precision=hi)

    local = gram_slots.reshape(1, 1, 64)
    sent = jnp.broadcast_to(jnp.pad(local, ((0, 0), (0, 0), (0, 64))), (128, 1, 128))
    parts = lax.all_to_all(sent, AXES, 0, 0, tiled=True)
    group_gram = jnp.sum(parts, axis=(0, 1))[:64].reshape(8, 8) / count
    scale = weights / jnp.sqrt(jnp.diagonal(group_gram) + 1e-06)

    def mixed(slots):
        return jnp.sum(scale[:, None, None] * slots.astype(F32), axis=0).astype(BF16)

    owned = jnp.concatenate([mixed(received) for received in slots], axis=1)
    left, right = jnp.split(owned, 2, axis=1)
    left = jnp.stack([left, shift(left, pair=1)])
    right = jnp.stack([right] + [shift(right, dz=n) for n in (1, 2, 3)])
    right = jnp.stack([right, shift(right, pair=1)], axis=1)
    left = jnp.stack([left] + [shift(left, dz=n) for n in (1, 2, 3)])
    pieces = jnp.concatenate([left, right], axis=3)
    combined = jnp.zeros((2 * HALF, WIN), BF16)
    for n in range(4):
        for b in range(2):
            row = (((z - n) % 4) * 2 + (x_lo ^ b)) * 32
            combined = lax.dynamic_update_slice(combined, pieces[n, b], (row, 0))
    gram = jnp.dot(jnp.dot(onehot.T, group_gram, precision=hi), onehot, precision=hi)
    return (combined, gram)


def solution(mesh):
    in_specs = (
        P(AXES, None),
        P(AXES, None),
        P("dom", "shard", None),
        P(),
        P(),
    )
    out_specs = (P("shard", None), P())
    return jax.shard_map(
        per_device, mesh=mesh, in_specs=in_specs, out_specs=out_specs, check_vma=False
    )
```

```python
import functools

import jax
import jax.numpy as jnp
from jax import lax
from jax.experimental import pallas as pl
from jax.experimental.pallas import tpu as pltpu
from jax.sharding import PartitionSpec as P

D_IN = 4096
WIN = 4096
AXES = ("dom", "shard")
EARLY = 1536
CHUNKS = (1024, 1536)
PIECES = ((0,), (1,))
HALF = 128
ORDER = ((0, 0), (0, 1), (1, 0), (3, 1), (2, 0), (1, 1), (2, 1), (3, 0))
PEERS = ((False, False), (False, True), (True, False), (True, True))
F32 = jnp.float32
BF16 = jnp.bfloat16


def device_index(x, y, z, core):
    return (z * 2 + x % 2) * 16 + (x // 2) * 8 + y * 2 + core


def shift(value, dx=0, dy=0, dz=0, pair=0, core=0):
    moves = [
        (
            device_index(x, y, z, c),
            device_index(((x ^ pair) + dx) % 4, (y + dy) % 4, (z + dz) % 4, c ^ core),
        )
        for x in range(4)
        for y in range(4)
        for z in range(4)
        for c in range(2)
    ]
    return lax.ppermute(value, AXES, moves)


def turn_kernel(at_ref, source, *outs):
    x_hi, y, core = at_ref[0], at_ref[1], at_ref[2]
    depth = source.shape[0]
    for out, (flip_x, flip_core) in zip(outs, PEERS):
        a = 1 - x_hi if flip_x else x_hi
        c = 1 - core if flip_core else core
        for i, (step, half) in enumerate(ORDER):
            block = ((a * 4 + lax.rem(y + step, 4)) * 2 + c) * 2 + half
            columns = pl.ds(pl.multiple_of(block * HALF, HALF), HALF)
            out[pl.ds(i % 2 * HALF, HALF), pl.ds(i // 2 * depth, depth)] = source[:, columns].T


def turned_columns(inputs, at):
    rows = inputs.shape[0]
    return pl.pallas_call(
        turn_kernel,
        in_specs=[
            pl.BlockSpec(memory_space=pltpu.SMEM),
            pl.BlockSpec(memory_space=pltpu.VMEM),
        ],
        out_specs=[pl.BlockSpec(memory_space=pltpu.VMEM)] * 4,
        out_shape=[jax.ShapeDtypeStruct((2 * HALF, 4 * rows), BF16)] * 4,
        compiler_params=pltpu.CompilerParams(vmem_limit_bytes=16 * 1024 * 1024),
        cost_estimate=pl.CostEstimate(
            flops=0, bytes_accessed=4 * inputs.size, transcendentals=0
        ),
    )(at, inputs)


def matmul_kernel(sets, terms, parts, *refs):
    operands, outs = refs[: (sets + 1) * terms], refs[(sets + 1) * terms :]
    lefts, rights = operands[: sets * terms], operands[sets * terms :]
    depth = rights[0].shape[0]
    for r in range(sets):
        for i, out in zip(parts, outs):
            total = None
            for left, right in zip(lefts[r * terms : (r + 1) * terms], rights):
                term = jnp.dot(
                    left[:, pl.ds(i * depth, depth)], right[...], preferred_element_type=F32
                )
                total = term if total is None else total + term
            out[r] = total.astype(BF16)


def block_products(sets, rights, width, parts=(0, 1, 2, 3)):
    rows, depth = 2 * HALF, rights[0][0].shape[0]
    tile = 512
    n, terms = len(sets), len(rights)
    lefts = sum(sets, [])

    def left_spec(offset):
        return pl.BlockSpec((rows, 4 * depth), lambda i: (0, offset // (4 * depth)))

    def right_spec(offset):
        return pl.BlockSpec((depth, tile), lambda i: (0, i + offset // tile))

    return pl.pallas_call(
        functools.partial(matmul_kernel, n, terms, parts),
        grid=(width // tile,),
        in_specs=[left_spec(o) for _, o in lefts] + [right_spec(o) for _, o in rights],
        out_specs=[pl.BlockSpec((n, rows, tile), lambda i: (0, 0, i))] * len(parts),
        out_shape=[jax.ShapeDtypeStruct((n, rows, width), BF16)] * len(parts),
        compiler_params=pltpu.CompilerParams(vmem_limit_bytes=32 * 1024 * 1024),
        cost_estimate=pl.CostEstimate(flops=0, bytes_accessed=0, transcendentals=0),
    )(*[v for v, _ in lefts], *[v for v, _ in rights])


def after(values, *done):
    out = lax.optimization_barrier((tuple(values), done))
    return out[0]


def finish_kernel(offset, ready, own, from_back, from_next, back2, next2, weight, out):
    before, width = ready.shape[1], own.shape[2]
    out[:, pl.ds(0, before)] = ready[...]
    for half, first, second in ((0, from_next, back2), (1, from_back, next2)):
        rows = pl.ds(half * HALF, HALF)
        total = own[0, rows, :].astype(F32) + second[0].astype(F32)
        total += first[0, pl.ds(HALF, HALF), :].astype(F32)
        scaled = total * weight[rows, pl.ds(offset, width)].astype(F32)
        out[rows, pl.ds(before, width)] = scaled.astype(BF16)


def finished(ready, second, weight, offset):
    whole = pl.BlockSpec(memory_space=pltpu.VMEM)
    width = ready.shape[1] + second[0].shape[2]
    return pl.pallas_call(
        functools.partial(finish_kernel, offset),
        in_specs=[whole] * 7,
        out_specs=whole,
        out_shape=jax.ShapeDtypeStruct((2 * HALF, width), BF16),
        compiler_params=pltpu.CompilerParams(vmem_limit_bytes=40 * 1024 * 1024),
        cost_estimate=pl.CostEstimate(flops=0, bytes_accessed=0, transcendentals=0),
    )(ready, *second, weight)


def add(a, b):
    return (a.astype(F32) + b.astype(F32)).astype(BF16)


def per_device(inputs, grads_out, domain_weight, domain_ids, mix_weights):
    dom = lax.axis_index("dom")
    shard = lax.axis_index("shard")
    z, x_lo = dom // 2, dom % 2
    x_hi, y, core = shard // 8, (shard // 2) % 4, shard % 2
    count = D_IN * WIN
    hi = lax.Precision.HIGHEST
    weight = domain_weight[0]

    n_chunks = len(CHUNKS)
    starts = [EARLY + sum(CHUNKS[:k]) for k in range(n_chunks)]
    ends = [start + width for start, width in zip(starts, CHUNKS)]
    spans = [(starts[piece[0]], ends[piece[-1]]) for piece in PIECES]
    own_left, core_left, x_left, both_left = turned_columns(inputs, jnp.stack([x_hi, y, core]))
    grads_core = shift(grads_out, core=1)
    core_left = shift(core_left, core=1)
    both_left = shift(both_left, core=1)
    own_set = [(own_left, 0), (core_left, 0)]
    other_set = [(x_left, 0), (both_left, 0)]
    sent = jnp.concatenate([x_left, both_left, grads_out[:, slice(*spans[0])]], axis=1)
    skip = 2 * x_left.shape[1]
    across = [shift(sent, dx=2)]
    lefts = own_set + [(across[0], 0), (across[0], skip // 2)]
    waits = [sent, across[0]]
    for p in range(1, len(PIECES)):
        (piece,) = after([grads_out[:, slice(*spans[p])]], waits[p - 1])
        across.append(shift(piece, dx=2))
        waits.append(across[-1])
    def reduce_first(products):
        own, keep, up, down = products
        return own, keep, shift(up, dy=1), shift(down, dy=-1)

    def reduce_second(first):
        own, keep, from_back, from_next = first
        sums = add(keep[:, :HALF], from_back[:, :HALF]), add(keep[:, HALF:], from_next[:, :HALF])
        return sums, (
            own, from_back, from_next, shift(sums[0], dy=1), shift(sums[1], dy=-1),
        )

    def reduce_last(second, *done):
        own, from_back, from_next, back2, next2 = after(second, *done)
        top = own[:, :HALF].astype(F32) + back2.astype(F32) + from_next[:, HALF:].astype(F32)
        bottom = own[:, HALF:].astype(F32) + from_back[:, HALF:].astype(F32) + next2.astype(F32)
        return jnp.concatenate([top, bottom], axis=1)

    def centered(weff_grad, start):
        block = weight[:, start : start + weff_grad.shape[1]].astype(F32)
        return (weff_grad * block).astype(BF16)

    def spread(*centers):
        pieces = jnp.concatenate(centers, axis=1)
        return lax.all_to_all(pieces.reshape(8, 32, -1), "dom", 0, 0, tiled=True)

    swapped = {}

    def products(k, *done, swap_after=()):
        p = next(p for p, piece in enumerate(PIECES) if k in piece)
        inner = starts[k] - spans[p][0]
        if p not in swapped:
            (far,) = after([across[p]], *(swap_after or done))
            swapped[p] = shift(far if p else far[:, skip:], core=1)
        far, far_core = after([across[p], swapped[p]], *done)
        rights = [
            (grads_out, starts[k]), (grads_core, starts[k]), (far, inner + (0 if p else skip)), (far_core, inner),
        ]
        return block_products([lefts], rights, CHUNKS[k])

    chip = [own_set, other_set], [(grads_out, 0), (grads_core, 0)]
    up, down = block_products(*chip, EARLY, (2, 3))
    grads, _ = after([grads_out, up])
    own, keep = block_products(chip[0], [(grads, 0), (grads_core, 0)], EARLY, (0, 1))
    first = reduce_first((own, keep, up, down))
    sums, early = reduce_second(first)

    def partial_gram(slots):
        flat = slots.reshape(8, -1)
        return lax.dot_general(flat, flat, (((1,), (1,)), ((), ())), preferred_element_type=F32)

    out0 = products(0, *sums)
    first0 = reduce_first(out0)
    out1 = products(1, out0[2], *early, swap_after=out0[2:3])
    early = reduce_last(early, out0[2])
    early_other = shift(early[1].astype(BF16), dx=2)
    first1 = reduce_first(out1)
    sums, second0 = reduce_second(after(first0, out1[2]))
    center_early = centered(early[0] + after([early_other], *sums)[0].astype(F32), 0)
    slots = [spread(center_early)]
    sums, second1 = reduce_second(after(first1, center_early))
    center0 = centered(reduce_last(second0, *sums)[0], starts[0])
    center = finished(center0, second1, weight, starts[1])
    slots.append(spread(after([center], slots[0])[0]))
    gram_slots = partial_gram(after([slots[0]], center)[0]) + partial_gram(slots[1])

    labels = jnp.arange(8, dtype=jnp.int32)
    onehot = (domain_ids[:, None] == labels[None, :]).astype(F32)
    weights = jnp.dot(onehot, mix_weights, precision=hi)

    local = gram_slots.reshape(1, 1, 64)
    sent = jnp.broadcast_to(jnp.pad(local, ((0, 0), (0, 0), (0, 64))), (128, 1, 128))
    parts = lax.all_to_all(sent, AXES, 0, 0, tiled=True)
    group_gram = jnp.sum(parts, axis=(0, 1))[:64].reshape(8, 8) / count
    scale = weights / jnp.sqrt(jnp.sum(jnp.where(labels[:, None] == labels[None, :], group_gram, 0.0), axis=1) + 1e-06)

    def mixed(slots):
        return jnp.sum(scale[:, None, None] * slots.astype(F32), axis=0).astype(BF16)

    left, right = (mixed(received) for received in slots)
    left = jnp.stack([left, shift(left, pair=1)])
    right = jnp.stack([right] + [shift(right, dz=n) for n in (1, 2, 3)])
    right = jnp.stack([right, shift(right, pair=1)], axis=1)
    left = jnp.stack([left] + [shift(left, dz=n) for n in (1, 2, 3)])
    pieces = jnp.concatenate([left, right], axis=3)
    combined = jnp.zeros((2 * HALF, WIN), BF16)
    for n in range(4):
        for b in range(2):
            row = (((z - n) % 4) * 2 + (x_lo ^ b)) * 32
            combined = lax.dynamic_update_slice(combined, pieces[n, b], (row, 0))
    gram = jnp.dot(jnp.dot(onehot.T, group_gram, precision=hi), onehot, precision=hi)
    return (combined, gram)


def solution(mesh):
    in_specs = (
        P(AXES, None),
        P(AXES, None),
        P("dom", "shard", None),
        P(),
        P(),
    )
    out_specs = (P("shard", None), P())
    return jax.shard_map(
        per_device, mesh=mesh, in_specs=in_specs, out_specs=out_specs, check_vma=False
    )
```

```python
import functools

import jax
import jax.numpy as jnp
from jax import lax
from jax.experimental import pallas as pl
from jax.experimental.pallas import tpu as pltpu
from jax.sharding import PartitionSpec as P

D_IN = 4096
WIN = 4096
AXES = ("dom", "shard")
EARLY = 1536
CHUNKS = (1024, 1536)
PIECES = ((0,), (1,))
HALF = 128
ORDER = ((0, 0), (0, 1), (1, 0), (3, 1), (2, 0), (1, 1), (2, 1), (3, 0))
PEERS = ((False, False), (False, True), (True, False), (True, True))
F32 = jnp.float32
BF16 = jnp.bfloat16


def device_index(x, y, z, core):
    return (z * 2 + x % 2) * 16 + (x // 2) * 8 + y * 2 + core


def shift(value, dx=0, dy=0, dz=0, pair=0, core=0):
    moves = [
        (
            device_index(x, y, z, c),
            device_index(((x ^ pair) + dx) % 4, (y + dy) % 4, (z + dz) % 4, c ^ core),
        )
        for x in range(4)
        for y in range(4)
        for z in range(4)
        for c in range(2)
    ]
    return lax.ppermute(value, AXES, moves)


def turn_kernel(at_ref, source, *outs):
    x_hi, y, core = at_ref[0], at_ref[1], at_ref[2]
    depth = source.shape[0]
    for out, (flip_x, flip_core) in zip(outs, PEERS):
        a = 1 - x_hi if flip_x else x_hi
        c = 1 - core if flip_core else core
        for i, (step, half) in enumerate(ORDER):
            block = ((a * 4 + lax.rem(y + step, 4)) * 2 + c) * 2 + half
            columns = pl.ds(pl.multiple_of(block * HALF, HALF), HALF)
            out[pl.ds(i % 2 * HALF, HALF), pl.ds(i // 2 * depth, depth)] = source[:, columns].T


def turned_columns(inputs, at):
    rows = inputs.shape[0]
    return pl.pallas_call(
        turn_kernel,
        in_specs=[
            pl.BlockSpec(memory_space=pltpu.SMEM),
            pl.BlockSpec(memory_space=pltpu.VMEM),
        ],
        out_specs=[pl.BlockSpec(memory_space=pltpu.VMEM)] * 4,
        out_shape=[jax.ShapeDtypeStruct((2 * HALF, 4 * rows), BF16)] * 4,
        compiler_params=pltpu.CompilerParams(vmem_limit_bytes=16 * 1024 * 1024),
        cost_estimate=pl.CostEstimate(
            flops=0, bytes_accessed=4 * inputs.size, transcendentals=0
        ),
    )(at, inputs)


def matmul_kernel(sets, terms, parts, *refs):
    operands, outs = refs[: (sets + 1) * terms], refs[(sets + 1) * terms :]
    lefts, rights = operands[: sets * terms], operands[sets * terms :]
    depth = rights[0].shape[0]
    for r in range(sets):
        for i, out in zip(parts, outs):
            total = None
            for left, right in zip(lefts[r * terms : (r + 1) * terms], rights):
                term = jnp.dot(
                    left[:, pl.ds(i * depth, depth)], right[...], preferred_element_type=F32
                )
                total = term if total is None else total + term
            out[r] = total.astype(BF16)


def block_products(sets, rights, width, parts=(0, 1, 2, 3)):
    rows, depth = 2 * HALF, rights[0][0].shape[0]
    tile = 512
    n, terms = len(sets), len(rights)
    lefts = sum(sets, [])

    def left_spec(offset):
        return pl.BlockSpec((rows, 4 * depth), lambda i: (0, offset // (4 * depth)))

    def right_spec(offset):
        return pl.BlockSpec((depth, tile), lambda i: (0, i + offset // tile))

    return pl.pallas_call(
        functools.partial(matmul_kernel, n, terms, parts),
        grid=(width // tile,),
        in_specs=[left_spec(o) for _, o in lefts] + [right_spec(o) for _, o in rights],
        out_specs=[pl.BlockSpec((n, rows, tile), lambda i: (0, 0, i))] * len(parts),
        out_shape=[jax.ShapeDtypeStruct((n, rows, width), BF16)] * len(parts),
        compiler_params=pltpu.CompilerParams(vmem_limit_bytes=32 * 1024 * 1024),
        cost_estimate=pl.CostEstimate(flops=0, bytes_accessed=0, transcendentals=0),
    )(*[v for v, _ in lefts], *[v for v, _ in rights])


def after(values, *done):
    out = lax.optimization_barrier((tuple(values), done))
    return out[0]


def finish_kernel(offset, ready, own, from_back, from_next, back2, next2, weight, out):
    before, width = ready.shape[1], own.shape[2]
    out[:, pl.ds(0, before)] = ready[...]
    for half, first, second in ((0, from_next, back2), (1, from_back, next2)):
        rows = pl.ds(half * HALF, HALF)
        total = own[0, rows, :].astype(F32) + second[0].astype(F32)
        total += first[0, pl.ds(HALF, HALF), :].astype(F32)
        scaled = total * weight[rows, pl.ds(offset, width)].astype(F32)
        out[rows, pl.ds(before, width)] = scaled.astype(BF16)


def finished(ready, second, weight, offset):
    whole = pl.BlockSpec(memory_space=pltpu.VMEM)
    width = ready.shape[1] + second[0].shape[2]
    return pl.pallas_call(
        functools.partial(finish_kernel, offset),
        in_specs=[whole] * 7,
        out_specs=whole,
        out_shape=jax.ShapeDtypeStruct((2 * HALF, width), BF16),
        compiler_params=pltpu.CompilerParams(vmem_limit_bytes=40 * 1024 * 1024),
        cost_estimate=pl.CostEstimate(flops=0, bytes_accessed=0, transcendentals=0),
    )(ready, *second, weight)


def add(a, b):
    return (a.astype(F32) + b.astype(F32)).astype(BF16)


def per_device(inputs, grads_out, domain_weight, domain_ids, mix_weights):
    dom = lax.axis_index("dom")
    shard = lax.axis_index("shard")
    z, x_lo = dom // 2, dom % 2
    x_hi, y, core = shard // 8, (shard // 2) % 4, shard % 2
    count = D_IN * WIN
    hi = lax.Precision.HIGHEST
    weight = domain_weight[0]

    n_chunks = len(CHUNKS)
    starts = [EARLY + sum(CHUNKS[:k]) for k in range(n_chunks)]
    ends = [start + width for start, width in zip(starts, CHUNKS)]
    spans = [(starts[piece[0]], ends[piece[-1]]) for piece in PIECES]
    own_left, core_left, x_left, both_left = turned_columns(inputs, jnp.stack([x_hi, y, core]))
    grads_core = shift(grads_out, core=1)
    core_left = shift(core_left, core=1)
    both_left = shift(both_left, core=1)
    own_set = [(own_left, 0), (core_left, 0)]
    other_set = [(x_left, 0), (both_left, 0)]
    sent = jnp.concatenate([x_left, both_left, grads_out[:, slice(*spans[0])]], axis=1)
    skip = 2 * x_left.shape[1]
    across = [shift(sent, dx=2)]
    lefts = own_set + [(across[0], 0), (across[0], skip // 2)]
    waits = [sent, across[0]]
    for p in range(1, len(PIECES)):
        (piece,) = after([grads_out[:, slice(*spans[p])]], waits[p - 1])
        across.append(shift(piece, dx=2))
        waits.append(across[-1])
    def reduce_first(products):
        own, keep, up, down = products
        return own, keep, shift(up, dy=1), shift(down, dy=-1)

    def reduce_second(first):
        own, keep, from_back, from_next = first
        sums = add(keep[:, :HALF], from_back[:, :HALF]), add(keep[:, HALF:], from_next[:, :HALF])
        return sums, (
            own, from_back, from_next, shift(sums[0], dy=1), shift(sums[1], dy=-1),
        )

    def reduce_last(second, *done):
        own, from_back, from_next, back2, next2 = after(second, *done)
        top = own[:, :HALF].astype(F32) + back2.astype(F32) + from_next[:, HALF:].astype(F32)
        bottom = own[:, HALF:].astype(F32) + from_back[:, HALF:].astype(F32) + next2.astype(F32)
        return jnp.concatenate([top, bottom], axis=1)

    def centered(weff_grad, start):
        block = weight[:, start : start + weff_grad.shape[1]].astype(F32)
        return (weff_grad * block).astype(BF16)

    def spread(*centers):
        pieces = jnp.concatenate(centers, axis=1)
        return lax.all_to_all(pieces.reshape(8, 32, -1), "dom", 0, 0, tiled=True)

    swapped = {}

    def products(k, *done, swap_after=()):
        p = next(p for p, piece in enumerate(PIECES) if k in piece)
        inner = starts[k] - spans[p][0]
        if p not in swapped:
            (far,) = after([across[p]], *(swap_after or done))
            swapped[p] = shift(far if p else far[:, skip:], core=1)
        far, far_core = after([across[p], swapped[p]], *done)
        rights = [
            (grads_out, starts[k]), (grads_core, starts[k]), (far, inner + (0 if p else skip)), (far_core, inner),
        ]
        return block_products([lefts], rights, CHUNKS[k])

    chip = [own_set, other_set], [(grads_out, 0), (grads_core, 0)]
    up, down = block_products(*chip, EARLY, (2, 3))
    grads, _ = after([grads_out, up])
    own, keep = block_products(chip[0], [(grads, 0), (grads_core, 0)], EARLY, (0, 1))
    first = reduce_first((own, keep, up, down))
    sums, early = reduce_second(first)

    def partial_gram(slots):
        flat = slots.reshape(8, -1)
        return lax.dot_general(flat, flat, (((1,), (1,)), ((), ())), preferred_element_type=F32)

    out0 = products(0, *sums)
    first0 = reduce_first(out0)
    out1 = products(1, out0[2], *early, swap_after=out0[2:3])
    early = reduce_last(early, out0[2])
    early_other = shift(early[1].astype(BF16), dx=2)
    first1 = reduce_first(out1)
    sums, second0 = reduce_second(after(first0, out1[2]))
    center_early = centered(early[0] + after([early_other], *sums)[0].astype(F32), 0)
    slots = [spread(center_early)]
    sums, second1 = reduce_second(after(first1, center_early))
    center0 = centered(reduce_last(second0, *sums)[0], starts[0])
    center = finished(center0, second1, weight, starts[1])
    slots.append(spread(after([center], slots[0])[0]))
    gram_slots = partial_gram(after([slots[0]], center)[0]) + partial_gram(slots[1])

    labels = jnp.arange(8, dtype=jnp.int32)
    onehot = (domain_ids[:, None] == labels[None, :]).astype(F32)
    weights = jnp.dot(onehot, mix_weights, precision=hi)

    local = gram_slots.reshape(1, 1, 64)
    sent = jnp.broadcast_to(jnp.pad(local, ((0, 0), (0, 0), (0, 64))), (128, 1, 128))
    parts = lax.all_to_all(sent, AXES, 0, 0, tiled=True)
    group_gram = jnp.sum(parts, axis=(0, 1))[:64].reshape(8, 8) / count
    scale = weights / jnp.sqrt(jnp.sum(jnp.where(labels[:, None] == labels[None, :], group_gram, 0.0), axis=1) + 1e-06)

    def mixed(slots):
        return jnp.sum(scale[:, None, None] * slots.astype(F32), axis=0).astype(BF16)

    left, right = (mixed(received) for received in slots)
    split = left.shape[1]
    other = shift(jnp.concatenate([left, right], axis=1), pair=1)
    around = jnp.stack([shift(right, dz=n) for n in (1, 2, 3)])
    crossed = shift(around, pair=1)
    left = jnp.stack([left, other[:, :split]])
    left = jnp.stack([left] + [shift(left, dz=n) for n in (1, 2, 3)])
    right = jnp.concatenate(
        [jnp.stack([right, other[:, split:]])[None], jnp.stack([around, crossed], axis=1)]
    )
    pieces = jnp.concatenate([left, right], axis=3)
    combined = jnp.zeros((2 * HALF, WIN), BF16)
    for n in range(4):
        for b in range(2):
            row = (((z - n) % 4) * 2 + (x_lo ^ b)) * 32
            combined = lax.dynamic_update_slice(combined, pieces[n, b], (row, 0))
    gram = jnp.dot(jnp.dot(onehot.T, group_gram, precision=hi), onehot, precision=hi)
    return (combined, gram)


def solution(mesh):
    in_specs = (
        P(AXES, None),
        P(AXES, None),
        P("dom", "shard", None),
        P(),
        P(),
    )
    out_specs = (P("shard", None), P())
    return jax.shard_map(
        per_device, mesh=mesh, in_specs=in_specs, out_specs=out_specs, check_vma=False
    )
```

```python
import functools

import jax
import jax.numpy as jnp
from jax import lax
from jax.experimental import pallas as pl
from jax.experimental.pallas import tpu as pltpu
from jax.sharding import PartitionSpec as P

D_IN = 4096
WIN = 4096
AXES = ("dom", "shard")
EARLY = 1536
CHUNKS = (1024, 1536)
PIECES = ((0,), (1,))
HALF = 128
FAR_FIRST = (2, 1, 3)
ORDER = ((0, 0), (0, 1), (1, 0), (3, 1), (2, 0), (1, 1), (2, 1), (3, 0))
PEERS = ((False, False), (False, True), (True, False), (True, True))
F32 = jnp.float32
BF16 = jnp.bfloat16


def device_index(x, y, z, core):
    return (z * 2 + x % 2) * 16 + (x // 2) * 8 + y * 2 + core


def shift(value, dx=0, dy=0, dz=0, pair=0, core=0):
    moves = [
        (
            device_index(x, y, z, c),
            device_index(((x ^ pair) + dx) % 4, (y + dy) % 4, (z + dz) % 4, c ^ core),
        )
        for x in range(4)
        for y in range(4)
        for z in range(4)
        for c in range(2)
    ]
    return lax.ppermute(value, AXES, moves)


def turn_kernel(at_ref, source, *outs):
    x_hi, y, core = at_ref[0], at_ref[1], at_ref[2]
    depth = source.shape[0]
    for out, (flip_x, flip_core) in zip(outs, PEERS):
        a = 1 - x_hi if flip_x else x_hi
        c = 1 - core if flip_core else core
        for i, (step, half) in enumerate(ORDER):
            block = ((a * 4 + lax.rem(y + step, 4)) * 2 + c) * 2 + half
            columns = pl.ds(pl.multiple_of(block * HALF, HALF), HALF)
            out[pl.ds(i % 2 * HALF, HALF), pl.ds(i // 2 * depth, depth)] = source[:, columns].T


def turned_columns(inputs, at):
    rows = inputs.shape[0]
    return pl.pallas_call(
        turn_kernel,
        in_specs=[
            pl.BlockSpec(memory_space=pltpu.SMEM),
            pl.BlockSpec(memory_space=pltpu.VMEM),
        ],
        out_specs=[pl.BlockSpec(memory_space=pltpu.VMEM)] * 4,
        out_shape=[jax.ShapeDtypeStruct((2 * HALF, 4 * rows), BF16)] * 4,
        compiler_params=pltpu.CompilerParams(vmem_limit_bytes=16 * 1024 * 1024),
        cost_estimate=pl.CostEstimate(
            flops=0, bytes_accessed=4 * inputs.size, transcendentals=0
        ),
    )(at, inputs)


def matmul_kernel(sets, terms, parts, *refs):
    operands, outs = refs[: (sets + 1) * terms], refs[(sets + 1) * terms :]
    lefts, rights = operands[: sets * terms], operands[sets * terms :]
    depth = rights[0].shape[0]
    for r in range(sets):
        for i, out in zip(parts, outs):
            total = None
            for left, right in zip(lefts[r * terms : (r + 1) * terms], rights):
                term = jnp.dot(
                    left[:, pl.ds(i * depth, depth)], right[...], preferred_element_type=F32
                )
                total = term if total is None else total + term
            out[r] = total.astype(BF16)


def message_kernel(n_left, parts, width, *refs):
    terms = n_left // 2
    rights, outs = refs[n_left : -len(parts)], refs[-len(parts) :]
    depth, tile = rights[0].shape[0], 512
    for start in range(0, width, tile):
        columns = pl.ds(start, tile)
        for r in range(2):
            for i, out in zip(parts, outs):
                total = None
                for left, right in zip(refs[r * terms : (r + 1) * terms], rights):
                    term = jnp.dot(
                        left[:, pl.ds(i * depth, depth)], right[:, columns], preferred_element_type=F32
                    )
                    total = term if total is None else total + term
                out[r, :, columns] = total.astype(BF16)


def message_products(lefts, rights, width, parts):
    whole = pl.BlockSpec(memory_space=pltpu.VMEM)
    return pl.pallas_call(
        functools.partial(message_kernel, len(lefts), parts, width),
        in_specs=[whole] * (len(lefts) + len(rights)),
        out_specs=[whole] * len(parts),
        out_shape=[jax.ShapeDtypeStruct((2, 2 * HALF, width), BF16)] * len(parts),
        compiler_params=pltpu.CompilerParams(vmem_limit_bytes=32 * 1024 * 1024),
        cost_estimate=pl.CostEstimate(flops=0, bytes_accessed=0, transcendentals=0),
    )(*lefts, *rights)


def block_products(sets, rights, width, parts=(0, 1, 2, 3)):
    rows, depth = 2 * HALF, rights[0][0].shape[0]
    tile = 512
    n, terms = len(sets), len(rights)
    lefts = sum(sets, [])

    def left_spec(offset):
        return pl.BlockSpec((rows, 4 * depth), lambda i: (0, offset // (4 * depth)))

    def right_spec(offset):
        return pl.BlockSpec((depth, tile), lambda i: (0, i + offset // tile))

    return pl.pallas_call(
        functools.partial(matmul_kernel, n, terms, parts),
        grid=(width // tile,),
        in_specs=[left_spec(o) for _, o in lefts] + [right_spec(o) for _, o in rights],
        out_specs=[pl.BlockSpec((n, rows, tile), lambda i: (0, 0, i))] * len(parts),
        out_shape=[jax.ShapeDtypeStruct((n, rows, width), BF16)] * len(parts),
        compiler_params=pltpu.CompilerParams(vmem_limit_bytes=32 * 1024 * 1024),
        cost_estimate=pl.CostEstimate(flops=0, bytes_accessed=0, transcendentals=0),
    )(*[v for v, _ in lefts], *[v for v, _ in rights])


def after(values, *done):
    out = lax.optimization_barrier((tuple(values), done))
    return out[0]


def finish_kernel(offset, ready, own, from_back, from_next, back2, next2, weight, out):
    before, width = ready.shape[1], own.shape[2]
    out[:, pl.ds(0, before)] = ready[...]
    for half, first, second in ((0, from_next, back2), (1, from_back, next2)):
        rows = pl.ds(half * HALF, HALF)
        total = own[0, rows, :].astype(F32) + second[0].astype(F32)
        total += first[0, pl.ds(HALF, HALF), :].astype(F32)
        scaled = total * weight[rows, pl.ds(offset, width)].astype(F32)
        out[rows, pl.ds(before, width)] = scaled.astype(BF16)


def finished(ready, second, weight, offset):
    whole = pl.BlockSpec(memory_space=pltpu.VMEM)
    width = ready.shape[1] + second[0].shape[2]
    return pl.pallas_call(
        functools.partial(finish_kernel, offset),
        in_specs=[whole] * 7,
        out_specs=whole,
        out_shape=jax.ShapeDtypeStruct((2 * HALF, width), BF16),
        compiler_params=pltpu.CompilerParams(vmem_limit_bytes=40 * 1024 * 1024),
        cost_estimate=pl.CostEstimate(flops=0, bytes_accessed=0, transcendentals=0),
    )(ready, *second, weight)


def add(a, b):
    return (a.astype(F32) + b.astype(F32)).astype(BF16)


def per_device(inputs, grads_out, domain_weight, domain_ids, mix_weights):
    dom = lax.axis_index("dom")
    shard = lax.axis_index("shard")
    z, x_lo = dom // 2, dom % 2
    x_hi, y, core = shard // 8, (shard // 2) % 4, shard % 2
    count = D_IN * WIN
    hi = lax.Precision.HIGHEST
    weight = domain_weight[0]

    n_chunks = len(CHUNKS)
    starts = [EARLY + sum(CHUNKS[:k]) for k in range(n_chunks)]
    ends = [start + width for start, width in zip(starts, CHUNKS)]
    spans = [(starts[piece[0]], ends[piece[-1]]) for piece in PIECES]
    own_left, core_left, x_left, both_left = turned_columns(inputs, jnp.stack([x_hi, y, core]))
    grads_core = shift(grads_out, core=1)
    core_left = shift(core_left, core=1)
    both_left = shift(both_left, core=1)
    own_set = [(own_left, 0), (core_left, 0)]
    other_set = [(x_left, 0), (both_left, 0)]
    sent = jnp.concatenate([x_left, both_left, grads_out[:, slice(*spans[0])]], axis=1)
    skip = 2 * x_left.shape[1]
    across = [shift(sent, dx=2)]
    lefts = own_set + [(across[0], 0), (across[0], skip // 2)]
    waits = [sent, across[0]]
    for p in range(1, len(PIECES)):
        (piece,) = after([grads_out[:, slice(*spans[p])]], waits[p - 1])
        across.append(shift(piece, dx=2))
        waits.append(across[-1])
    def reduce_first(products):
        own, keep, up, down = products
        return own, keep, shift(up, dy=1), shift(down, dy=-1)

    def reduce_second(first):
        own, keep, from_back, from_next = first
        sums = add(keep[:, :HALF], from_back[:, :HALF]), add(keep[:, HALF:], from_next[:, :HALF])
        return sums, (
            own, from_back, from_next, shift(sums[0], dy=1), shift(sums[1], dy=-1),
        )

    def reduce_last(second, *done):
        own, from_back, from_next, back2, next2 = after(second, *done)
        top = own[:, :HALF].astype(F32) + back2.astype(F32) + from_next[:, HALF:].astype(F32)
        bottom = own[:, HALF:].astype(F32) + from_back[:, HALF:].astype(F32) + next2.astype(F32)
        return jnp.concatenate([top, bottom], axis=1)

    def centered(weff_grad, start):
        block = weight[:, start : start + weff_grad.shape[1]].astype(F32)
        return (weff_grad * block).astype(BF16)

    def spread(*centers):
        pieces = jnp.concatenate(centers, axis=1)
        return lax.all_to_all(pieces.reshape(8, 32, -1), "dom", 0, 0, tiled=True)

    swapped = {}

    def products(k, *done, swap_after=()):
        p = next(p for p, piece in enumerate(PIECES) if k in piece)
        inner = starts[k] - spans[p][0]
        if p not in swapped:
            (far,) = after([across[p]], *(swap_after or done))
            swapped[p] = shift(far if p else far[:, skip:], core=1)
        far, far_core = after([across[p], swapped[p]], *done)
        rights = [
            (grads_out, starts[k]), (grads_core, starts[k]), (far, inner + (0 if p else skip)), (far_core, inner),
        ]
        return block_products([lefts], rights, CHUNKS[k])

    chip = [own_set, other_set], [(grads_out, 0), (grads_core, 0)]
    up, down = message_products(
        [own_left, core_left, x_left, both_left], [grads_out, grads_core], EARLY, (2, 3)
    )
    grads, _ = after([grads_out, up])
    own, keep = block_products(chip[0], [(grads, 0), (grads_core, 0)], EARLY, (0, 1))
    first = reduce_first((own, keep, up, down))
    sums, early = reduce_second(first)

    def partial_gram(slots):
        flat = slots.reshape(8, -1)
        return lax.dot_general(flat, flat, (((1,), (1,)), ((), ())), preferred_element_type=F32)

    out0 = products(0, *sums)
    first0 = reduce_first(out0)
    out1 = products(1, out0[2], *early, swap_after=out0[2:3])
    early = reduce_last(early, out0[2])
    early_other = shift(early[1].astype(BF16), dx=2)
    first1 = reduce_first(out1)
    sums, second0 = reduce_second(after(first0, out1[2]))
    center_early = centered(early[0] + after([early_other], *sums)[0].astype(F32), 0)
    slots = [spread(center_early)]
    sums, second1 = reduce_second(after(first1, center_early))
    center0 = centered(reduce_last(second0, *sums)[0], starts[0])
    center = finished(center0, second1, weight, starts[1])
    slots.append(spread(after([center], slots[0])[0]))
    gram_slots = partial_gram(after([slots[0]], center)[0]) + partial_gram(slots[1])

    labels = jnp.arange(8, dtype=jnp.int32)
    onehot = (domain_ids[:, None] == labels[None, :]).astype(F32)
    weights = jnp.dot(onehot, mix_weights, precision=hi)

    local = gram_slots.reshape(1, 1, 64)
    sent = jnp.broadcast_to(jnp.pad(local, ((0, 0), (0, 0), (0, 64))), (128, 1, 128))
    parts = lax.all_to_all(sent, AXES, 0, 0, tiled=True)
    group_gram = jnp.sum(parts, axis=(0, 1))[:64].reshape(8, 8) / count
    scale = weights / jnp.sqrt(jnp.sum(jnp.where(labels[:, None] == labels[None, :], group_gram, 0.0), axis=1) + 1e-06)

    def mixed(slots):
        return jnp.sum(scale[:, None, None] * slots.astype(F32), axis=0).astype(BF16)

    left, right = (mixed(received) for received in slots)
    split = left.shape[1]
    other = shift(jnp.concatenate([left, right], axis=1), pair=1)
    around = jnp.stack([shift(right, dz=n) for n in FAR_FIRST])
    crossed = shift(around, pair=1)
    left = jnp.stack([left, other[:, :split]])
    left = jnp.stack([left] + [shift(left, dz=n) for n in FAR_FIRST])
    right = jnp.concatenate(
        [jnp.stack([right, other[:, split:]])[None], jnp.stack([around, crossed], axis=1)]
    )
    pieces = jnp.concatenate([left, right], axis=3)
    combined = jnp.zeros((2 * HALF, WIN), BF16)
    for slot, n in enumerate((0, *FAR_FIRST)):
        for b in range(2):
            row = (((z - n) % 4) * 2 + (x_lo ^ b)) * 32
            combined = lax.dynamic_update_slice(combined, pieces[slot, b], (row, 0))
    gram = jnp.dot(jnp.dot(onehot.T, group_gram, precision=hi), onehot, precision=hi)
    return (combined, gram)


def solution(mesh):
    in_specs = (
        P(AXES, None),
        P(AXES, None),
        P("dom", "shard", None),
        P(),
        P(),
    )
    out_specs = (P("shard", None), P())
    return jax.shard_map(
        per_device, mesh=mesh, in_specs=in_specs, out_specs=out_specs, check_vma=False
    )
```
